512 devices in a mesh: row: 32 (over z, y_hi), col: 16 (over y_lo, x, core).
Axes of the slice: x: 4, y: 4 (y_hi: 2, y_lo: 2; y = y_hi * 2 + y_lo), z: 16, core: 2. Of those that a mesh axis runs over, the one named last changes fastest.
Arguments:
- doc_feats: float32 [1024, 16384], P('row', 'col'), may hold values from -6 to 6
- kernel_inv: float32 [16384, 16384], P('row', 'col'), may hold values from -0.046875 to 0.046875
- target_feats: float32 [256, 16384], P('row'), may hold values from -0.046875 to 0.046875
- doc_weight: float32 [1024], P('row'), may hold values from 0.1 to 1
Outputs:
- scores: float32 [1024, 256], P(('row', 'col'))
The draws below stay inside these ranges and needn't reach their ends.
All inputs are finite; a program needn't handle non-finite values.
Results may differ from the reference program's by a relative error of at most 0.000094.
Values sent between devices are 32-bit elements; how exact they have to be, the bound alone decides.
No kernel may reach another device: no remote copies, remote signals or barrier semaphores. Data moves between devices by JAX's collectives and lax.ppermute only.
A program may use at most 64 MiB of HBM per device.

```python
import jax
import jax.numpy as jnp
from jax import lax

P_SIZE = 16384
NDOC = 1024
NT = 256


def level_of(rng, dims, split, low, top_value):
    gain = 1.0
    for dim, parts in split:
        steps = jax.random.uniform(jax.random.fold_in(jax.random.fold_in(rng, 6), dim), (parts,), jnp.float32, low / len(split), top_value / len(split))
        gain = gain * jnp.repeat(jnp.exp(steps), dims[dim] // parts).reshape((-1,) + (1,) * (len(dims) - 1 - dim))
    return gain


def bell_draw(stream_key, dims, scale, limit, cuts=(), dtype=jnp.bfloat16):
    gain = level_of(stream_key, dims, cuts, -0.22, 0.18) if cuts else 1.0
    array = jax.random.normal(stream_key, dims, jnp.float32) * scale * gain
    return jnp.minimum(jnp.maximum(array, -limit), limit).astype(dtype)


def setup_inputs(seed: int = 0) -> dict:
    keys = jax.random.split(jax.random.key(seed), 5)
    return {
        "doc_feats": bell_draw(keys[0], (NDOC, P_SIZE), 1.0, 6.0, ((0, 32), (1, 16)), jnp.float32),
        "kernel_inv": bell_draw(keys[1], (P_SIZE, P_SIZE), P_SIZE ** -0.5, 0.046875, ((0, 32), (1, 16)), jnp.float32),
        "target_feats": bell_draw(keys[2], (NT, P_SIZE), P_SIZE ** -0.5, 0.046875, ((0, 32),), jnp.float32),
        "doc_weight": jnp.clip(0.1 + 0.9 * jax.random.uniform(keys[3], (NDOC,), jnp.float32) ** level_of(keys[3], (NDOC,), ((0, 32),), -0.2, 0.2), 0.1, 1.0),
    }


def reference(doc_feats, kernel_inv, target_feats, doc_weight):
    weighted = lax.dot_general(doc_feats, kernel_inv, (((1,), (1,)), ((), ())), precision=lax.Precision.HIGHEST, preferred_element_type=jnp.float32)
    raw = lax.dot_general(weighted, target_feats, (((1,), (1,)), ((), ())), precision=lax.Precision.HIGHEST, preferred_element_type=jnp.float32)
    return raw * doc_weight[:, None]
```

```python
import functools

import jax
import jax.numpy as jnp
from jax import lax
from jax.experimental import pallas as pl
from jax.experimental.pallas import tpu as pltpu
from jax.sharding import Mesh, PartitionSpec as P

NEAR = 4
VMEM = pl.BlockSpec(memory_space=pltpu.VMEM)
SMEM = pl.BlockSpec(memory_space=pltpu.SMEM)
PARAMS = pltpu.CompilerParams(vmem_limit_bytes=24 * 2**20)


def exchange(pieces, axis):
    return lax.all_to_all(pieces, axis, split_axis=0, concat_axis=0, tiled=True)


def split(x):
    hi = x.astype(jnp.bfloat16)
    return hi, (x - hi.astype(jnp.float32)).astype(jnp.bfloat16)


def dot3(left, right, left_dim, right_dim):
    def one(a, b):
        return lax.dot_general(
            a, b, (((left_dim,), (right_dim,)), ((), ())), preferred_element_type=jnp.float32
        )

    return one(left[0], right[0]) + (one(left[0], right[1]) + one(left[1], right[0]))


def cost(flops, size):
    return pl.CostEstimate(flops=flops, bytes_accessed=size, transcendentals=0)


def split_inverse(kernel_inv):
    n_i, n_j = kernel_inv.shape
    steps = 4

    def body(k_ref, hi_ref, lo_ref):
        hi_ref[...], lo_ref[...] = split(k_ref[...])

    block = pl.BlockSpec((n_i // steps, n_j), lambda s: (s, 0))
    half = jax.ShapeDtypeStruct((n_i, n_j), jnp.bfloat16)
    return pl.pallas_call(
        body,
        grid=(steps,),
        in_specs=[block],
        out_specs=[block, block],
        out_shape=[half, half],
        compiler_params=PARAMS,
        cost_estimate=cost(n_i * n_j * 4, n_i * n_j * 8),
        name="split_inverse",
    )(kernel_inv)


def mix_targets(core, mine, other, k_hi, k_lo):
    all_t, half = mine.shape
    n_j = k_hi.shape[1]
    sub = n_j // NEAR

    def body(core_ref, mine_ref, other_ref, hi_ref, lo_ref, out_ref):
        place = core_ref[0]
        sides = [(split(mine_ref[...]), place), (split(other_ref[...]), 1 - place)]
        for a in range(NEAR):
            cut = slice(a * sub, (a + 1) * sub)
            total = None
            for t, at in sides:
                rows = pl.ds(pl.multiple_of(at * half, half), half)
                part = dot3(t, (hi_ref[rows, cut], lo_ref[rows, cut]), 1, 0)
                total = part if total is None else total + part
            out_ref[a] = total

    return pl.pallas_call(
        body,
        in_specs=[SMEM, VMEM, VMEM, VMEM, VMEM],
        out_specs=VMEM,
        out_shape=jax.ShapeDtypeStruct((NEAR, all_t, sub), jnp.float32),
        compiler_params=PARAMS,
        cost_estimate=cost(6 * all_t * 2 * half * n_j, 4 * 2**20),
        name="mix_targets",
    )(core, mine, other, k_hi, k_lo)


def split_docs(docs, far, chips):
    n, width = docs.shape
    group = n // far // chips

    def body(x_ref, hi_ref, lo_ref):
        x = x_ref[...].reshape(far * group, width)
        hi_ref[...], lo_ref[...] = split(x)

    out = pl.BlockSpec((far * group, width), lambda s: (s, 0))
    half = jax.ShapeDtypeStruct((n, width), jnp.bfloat16)
    return pl.pallas_call(
        body,
        grid=(chips,),
        in_specs=[pl.BlockSpec((far, None, group, width), lambda s: (0, s, 0, 0))],
        out_specs=[out, out],
        out_shape=[half, half],
        compiler_params=PARAMS,
        cost_estimate=cost(2**38, 4 * n * width),
        name="split_docs",
    )(docs.reshape(far, chips, group, width))


def score_docs(d_hi, d_lo, mixed, pair):
    n, width = d_hi.shape
    all_t, sub = mixed.shape

    def body(hi_ref, lo_ref, mixed_ref, pair_ref, out_ref):
        near = dot3((hi_ref[:, :sub], lo_ref[:, :sub]), split(mixed_ref[...]), 1, 1)
        out_ref[...] = near + dot3((hi_ref[:, sub:], lo_ref[:, sub:]), split(pair_ref[...]), 1, 1)

    return pl.pallas_call(
        body,
        in_specs=[VMEM] * 4,
        out_specs=VMEM,
        out_shape=jax.ShapeDtypeStruct((n, all_t), jnp.float32),
        compiler_params=PARAMS,
        cost_estimate=cost(6 * n * width * all_t, 2 * 2**20),
        name="score_docs",
    )(d_hi, d_lo, mixed, pair)


def solution(mesh):
    rows, cols = mesh.shape["row"], mesh.shape["col"]
    far, chips = rows // NEAR, cols // 2
    names = ("far", "near", "chip", "core")
    fine = Mesh(mesh.devices.reshape(far, NEAR, chips, 2), names)
    row, col = ("far", "near"), ("chip", "core")
    swap = [(0, 1), (1, 0)]

    def on_device(doc_feats, kernel_inv, target_feats, doc_weight):
        core = lax.axis_index("core")
        n_t, p = target_feats.shape
        n_i, n_j = kernel_inv.shape
        n_d = doc_feats.shape[0]
        half, sub, own = n_i // 2, n_j // NEAR, n_d // cols
        all_t = rows * n_t

        docs = doc_feats.reshape(chips, 2, own, NEAR, sub).transpose(3, 1, 0, 2, 4)
        docs = exchange(docs.reshape(NEAR * 2, chips * own, sub), ("near", "core"))
        docs = docs.reshape(NEAR, 2, chips, own, sub)
        docs = jnp.where(core == 0, docs, docs[:, ::-1])
        docs = docs.transpose(2, 0, 3, 1, 4).reshape(chips * NEAR * own, 2 * sub)

        cut = target_feats.reshape(n_t, rows, 2, half)
        cut = lax.dynamic_index_in_dim(cut, core, 2, keepdims=False).transpose(1, 0, 2)
        docs, cut = lax.optimization_barrier((docs, cut))
        docs = lax.all_gather(docs, "far", axis=0, tiled=True)
        d_hi, d_lo = split_docs(docs, far, chips)

        k_hi, k_lo = split_inverse(kernel_inv)
        mine = exchange(cut, row).reshape(all_t, half)
        other = lax.ppermute(mine, "core", swap)
        mixed = mix_targets(core.reshape(1), mine, other, k_hi, k_lo)
        mixed = exchange(mixed, "near").sum(0)
        mixed, d_hi, d_lo = lax.optimization_barrier((mixed, d_hi, d_lo))
        pair = lax.ppermute(mixed, "core", swap)

        terms = score_docs(d_hi, d_lo, mixed, pair)
        terms = exchange(terms.reshape(chips, rows * own, all_t), "chip").sum(0)
        scores = exchange(terms.reshape(rows, own, all_t), row).sum(0)
        place = lax.axis_index("chip") * 2 + core
        own_weight = lax.dynamic_slice_in_dim(doc_weight, place * own, own, 0)
        return scores * own_weight[:, None]

    in_specs = (P(row, col), P(row, col), P(row, None), P(row))
    return jax.shard_map(
        on_device, mesh=fine, in_specs=in_specs, out_specs=P(row + col, None), check_vma=False
    )
```

```python
import functools

import jax
import jax.numpy as jnp
from jax import lax
from jax.experimental import pallas as pl
from jax.experimental.pallas import tpu as pltpu
from jax.sharding import Mesh, PartitionSpec as P

NEAR = 4
VMEM = pl.BlockSpec(memory_space=pltpu.VMEM)
SMEM = pl.BlockSpec(memory_space=pltpu.SMEM)
PARAMS = pltpu.CompilerParams(vmem_limit_bytes=24 * 2**20)


def exchange(pieces, axis):
    return lax.all_to_all(pieces, axis, split_axis=0, concat_axis=0, tiled=True)


def split(x):
    hi = x.astype(jnp.bfloat16)
    return hi, (x - hi.astype(jnp.float32)).astype(jnp.bfloat16)


def dot3(left, right, left_dim, right_dim):
    def one(a, b):
        return lax.dot_general(
            a, b, (((left_dim,), (right_dim,)), ((), ())), preferred_element_type=jnp.float32
        )

    return one(left[0], right[0]) + (one(left[0], right[1]) + one(left[1], right[0]))


def cost(flops, size):
    return pl.CostEstimate(flops=flops, bytes_accessed=size, transcendentals=0)


def split_inverse(kernel_inv):
    n_i, n_j = kernel_inv.shape
    steps = 4

    def body(k_ref, hi_ref, lo_ref):
        hi_ref[...], lo_ref[...] = split(k_ref[...])

    block = pl.BlockSpec((n_i // steps, n_j), lambda s: (s, 0))
    half = jax.ShapeDtypeStruct((n_i, n_j), jnp.bfloat16)
    return pl.pallas_call(
        body,
        grid=(steps,),
        in_specs=[block],
        out_specs=[block, block],
        out_shape=[half, half],
        compiler_params=PARAMS,
        cost_estimate=cost(n_i * n_j * 4, n_i * n_j * 8),
        name="split_inverse",
    )(kernel_inv)


def mix_targets(core, mine, other, k_hi, k_lo):
    all_t, half = mine.shape
    n_j = k_hi.shape[1]
    sub = n_j // NEAR

    def body(core_ref, mine_ref, other_ref, hi_ref, lo_ref, out_ref):
        place = core_ref[0]
        sides = [(split(mine_ref[...]), place), (split(other_ref[...]), 1 - place)]
        for a in range(NEAR):
            cut = slice(a * sub, (a + 1) * sub)
            total = None
            for t, at in sides:
                rows = pl.ds(pl.multiple_of(at * half, half), half)
                part = dot3(t, (hi_ref[rows, cut], lo_ref[rows, cut]), 1, 0)
                total = part if total is None else total + part
            out_ref[a] = total

    return pl.pallas_call(
        body,
        in_specs=[SMEM, VMEM, VMEM, VMEM, VMEM],
        out_specs=VMEM,
        out_shape=jax.ShapeDtypeStruct((NEAR, all_t, sub), jnp.float32),
        compiler_params=PARAMS,
        cost_estimate=cost(6 * all_t * 2 * half * n_j, 4 * 2**20),
        name="mix_targets",
    )(core, mine, other, k_hi, k_lo)


def split_docs(place, blocks, cols):
    near = len(blocks)
    each, width = blocks[0].shape
    own = each // cols
    group, n = near * own, near * each

    def body(place_ref, *refs):
        hi_ref, lo_ref, f32_ref = refs[near:]
        for s in range(near):
            for k in range(own):
                at = pl.ds(place_ref[s] * own + k, cols, stride=group)
                f32_ref[at, :] = refs[s][pl.ds(k, cols, stride=own), :]
        hi_ref[...], lo_ref[...] = split(f32_ref[...])

    lanes = 128
    out = pl.BlockSpec((n, lanes), lambda s: (0, s))
    half = jax.ShapeDtypeStruct((n, width), jnp.bfloat16)
    return pl.pallas_call(
        body,
        grid=(width // lanes,),
        in_specs=[SMEM] + [pl.BlockSpec((each, lanes), lambda s: (0, s))] * near,
        out_specs=[out, out],
        out_shape=[half, half],
        scratch_shapes=[pltpu.VMEM((n, lanes), jnp.float32)],
        compiler_params=PARAMS,
        cost_estimate=cost(4 * n * width, 8 * n * width),
        name="split_docs",
    )(place, *blocks)


def sum_copies(parts):
    n, some_t, sub = parts.shape

    def body(x_ref, out_ref):
        total = x_ref[0] + x_ref[1]
        for a in range(2, n):
            total = total + x_ref[a]
        for a in range(n):
            out_ref[a] = total

    return pl.pallas_call(
        body,
        in_specs=[VMEM],
        out_specs=VMEM,
        out_shape=jax.ShapeDtypeStruct(parts.shape, jnp.float32),
        compiler_params=PARAMS,
        cost_estimate=cost(n * some_t * sub, 8 * n * some_t * sub),
        name="sum_copies",
    )(parts)


def score_docs(d_hi, d_lo, mixed):
    n, width = d_hi.shape
    all_t = mixed.shape[0]

    def body(hi_ref, lo_ref, mixed_ref, out_ref):
        out_ref[...] = dot3((hi_ref[...], lo_ref[...]), split(mixed_ref[...]), 1, 1)

    return pl.pallas_call(
        body,
        in_specs=[VMEM] * 3,
        out_specs=VMEM,
        out_shape=jax.ShapeDtypeStruct((n, all_t), jnp.float32),
        compiler_params=PARAMS,
        cost_estimate=cost(6 * n * width * all_t, 2**20),
        name="score_docs",
    )(d_hi, d_lo, mixed)


def solution(mesh):
    rows, cols = mesh.shape["row"], mesh.shape["col"]
    far, chips = rows // NEAR, cols // 2
    names = ("far", "near", "chip", "core")
    fine = Mesh(mesh.devices.reshape(far, NEAR, chips, 2), names)
    row, col = ("far", "near"), ("chip", "core")
    swap = [(0, 1), (1, 0)]

    def on_device(doc_feats, kernel_inv, target_feats, doc_weight):
        core = lax.axis_index("core")
        n_t, p = target_feats.shape
        n_i, n_j = kernel_inv.shape
        n_d = doc_feats.shape[0]
        half, sub, own = n_i // 2, n_j // NEAR, n_d // cols
        all_t = rows * n_t

        cut = target_feats.reshape(n_t, rows, 2, half)
        cut = lax.dynamic_index_in_dim(cut, core, 2, keepdims=False).transpose(1, 0, 2)
        mine = exchange(cut, row).reshape(all_t, half)
        k_hi, k_lo = split_inverse(kernel_inv)

        here = lax.axis_index("near")
        place = jnp.stack([here ^ s for s in range(NEAR)])
        blocks = []
        for s in range(NEAR):
            block = lax.dynamic_slice_in_dim(doc_feats, place[s] * sub, sub, 1)
            pairs = [(a, a ^ s) for a in range(NEAR)]
            blocks.append(lax.ppermute(block, "near", pairs) if s else block)
        d_hi, d_lo = split_docs(place, blocks, cols)
        mine, k_hi, k_lo, d_hi, d_lo = lax.optimization_barrier((mine, k_hi, k_lo, d_hi, d_lo))

        other = lax.ppermute(mine, "core", swap)
        mixed = mix_targets(core.reshape(1), mine, other, k_hi, k_lo)
        mixed = exchange(mixed, "near").sum(0)
        mixed = exchange(mixed.reshape(far, all_t // far, sub), "far")
        mixed = exchange(sum_copies(mixed), "far").reshape(all_t, sub)

        terms = score_docs(d_hi, d_lo, mixed)
        terms = exchange(terms.reshape(cols, NEAR * own, all_t), col).sum(0)
        scores = exchange(terms.reshape(NEAR, own, all_t), "near").sum(0)
        place = lax.axis_index("chip") * 2 + core
        own_weight = lax.dynamic_slice_in_dim(doc_weight, place * own, own, 0)
        return scores * own_weight[:, None]

    in_specs = (P(row, col), P(row, col), P(row, None), P(row))
    return jax.shard_map(
        on_device, mesh=fine, in_specs=in_specs, out_specs=P(row + col, None), check_vma=False
    )
```

```python
import functools

import jax
import jax.numpy as jnp
from jax import lax
from jax.experimental import pallas as pl
from jax.experimental.pallas import tpu as pltpu
from jax.sharding import Mesh, PartitionSpec as P

NEAR = 4
VMEM = pl.BlockSpec(memory_space=pltpu.VMEM)
SMEM = pl.BlockSpec(memory_space=pltpu.SMEM)
PARAMS = pltpu.CompilerParams(vmem_limit_bytes=24 * 2**20)


def exchange(pieces, axis):
    return lax.all_to_all(pieces, axis, split_axis=0, concat_axis=0, tiled=True)


def split(x):
    hi = x.astype(jnp.bfloat16)
    return hi, (x - hi.astype(jnp.float32)).astype(jnp.bfloat16)


def dot3(left, right, left_dim, right_dim):
    def one(a, b):
        return lax.dot_general(
            a, b, (((left_dim,), (right_dim,)), ((), ())), preferred_element_type=jnp.float32
        )

    return one(left[0], right[0]) + (one(left[0], right[1]) + one(left[1], right[0]))


def cost(flops, size):
    return pl.CostEstimate(flops=flops, bytes_accessed=size, transcendentals=0)


def split_inverse(kernel_inv):
    n_i, n_j = kernel_inv.shape
    steps = 4

    def body(k_ref, hi_ref, lo_ref):
        hi_ref[...], lo_ref[...] = split(k_ref[...])

    block = pl.BlockSpec((n_i // steps, n_j), lambda s: (s, 0))
    half = jax.ShapeDtypeStruct((n_i, n_j), jnp.bfloat16)
    return pl.pallas_call(
        body,
        grid=(steps,),
        in_specs=[block],
        out_specs=[block, block],
        out_shape=[half, half],
        compiler_params=PARAMS,
        cost_estimate=cost(n_i * n_j * 4, n_i * n_j * 8),
        name="split_inverse",
    )(kernel_inv)


def mix_targets(core, mine, other, k_hi, k_lo):
    all_t, half = mine.shape
    n_j = k_hi.shape[1]
    sub = n_j // NEAR

    def body(core_ref, mine_ref, other_ref, hi_ref, lo_ref, out_ref):
        place = core_ref[0]
        sides = [(split(mine_ref[...]), place), (split(other_ref[...]), 1 - place)]
        for a in range(NEAR):
            cut = slice(a * sub, (a + 1) * sub)
            total = None
            for t, at in sides:
                rows = pl.ds(pl.multiple_of(at * half, half), half)
                part = dot3(t, (hi_ref[rows, cut], lo_ref[rows, cut]), 1, 0)
                total = part if total is None else total + part
            out_ref[a] = total

    return pl.pallas_call(
        body,
        in_specs=[SMEM, VMEM, VMEM, VMEM, VMEM],
        out_specs=VMEM,
        out_shape=jax.ShapeDtypeStruct((NEAR, all_t, sub), jnp.float32),
        compiler_params=PARAMS,
        cost_estimate=cost(6 * all_t * 2 * half * n_j, 4 * 2**20),
        name="mix_targets",
    )(core, mine, other, k_hi, k_lo)


def split_docs(place, blocks):
    near = len(blocks)
    each, width = blocks[0].shape

    def body(place_ref, *refs):
        hi_ref, lo_ref = refs[near:]
        for s in range(near):
            at = pl.ds(pl.multiple_of(place_ref[s] * each, each), each)
            hi_ref[at, :], lo_ref[at, :] = split(refs[s][...])

    half = jax.ShapeDtypeStruct((near * each, width), jnp.bfloat16)
    return pl.pallas_call(
        body,
        in_specs=[SMEM] + [VMEM] * near,
        out_specs=[VMEM, VMEM],
        out_shape=[half, half],
        compiler_params=PARAMS,
        cost_estimate=cost(4 * near * each * width, 8 * near * each * width),
        name="split_docs",
    )(place, *blocks)


def sum_copies(parts):
    n, some_t, sub = parts.shape

    def body(x_ref, out_ref):
        total = x_ref[0] + x_ref[1]
        for a in range(2, n):
            total = total + x_ref[a]
        for a in range(n):
            out_ref[a] = total

    return pl.pallas_call(
        body,
        in_specs=[VMEM],
        out_specs=VMEM,
        out_shape=jax.ShapeDtypeStruct(parts.shape, jnp.float32),
        compiler_params=PARAMS,
        cost_estimate=cost(n * some_t * sub, 8 * n * some_t * sub),
        name="sum_copies",
    )(parts)


def score_docs(d_hi, d_lo, mixed):
    n, width = d_hi.shape
    all_t = mixed.shape[0]

    def body(hi_ref, lo_ref, mixed_ref, out_ref):
        out_ref[...] = dot3((hi_ref[...], lo_ref[...]), split(mixed_ref[...]), 1, 1)

    return pl.pallas_call(
        body,
        in_specs=[VMEM] * 3,
        out_specs=VMEM,
        out_shape=jax.ShapeDtypeStruct((n, all_t), jnp.float32),
        compiler_params=PARAMS,
        cost_estimate=cost(6 * n * width * all_t, 2**20),
        name="score_docs",
    )(d_hi, d_lo, mixed)


def solution(mesh):
    rows, cols = mesh.shape["row"], mesh.shape["col"]
    far, chips = rows // NEAR, cols // 2
    names = ("far", "near", "chip", "core")
    fine = Mesh(mesh.devices.reshape(far, NEAR, chips, 2), names)
    row, col = ("far", "near"), ("chip", "core")
    swap = [(0, 1), (1, 0)]

    def on_device(doc_feats, kernel_inv, target_feats, doc_weight):
        core = lax.axis_index("core")
        n_t, p = target_feats.shape
        n_i, n_j = kernel_inv.shape
        n_d = doc_feats.shape[0]
        half, sub, own = n_i // 2, n_j // NEAR, n_d // cols
        all_t = rows * n_t

        cut = target_feats.reshape(n_t, rows, 2, half)
        cut = lax.dynamic_index_in_dim(cut, core, 2, keepdims=False).transpose(1, 0, 2)
        mine = exchange(cut, row).reshape(all_t, half)
        k_hi, k_lo = split_inverse(kernel_inv)

        here = lax.axis_index("near")
        place = jnp.stack([here ^ s for s in range(NEAR)])
        blocks = []
        for s in range(NEAR):
            block = lax.dynamic_slice_in_dim(doc_feats, place[s] * sub, sub, 1)
            pairs = [(a, a ^ s) for a in range(NEAR)]
            blocks.append(lax.ppermute(block, "near", pairs) if s else block)
        d_hi, d_lo = split_docs(place, blocks)
        mine, k_hi, k_lo, d_hi, d_lo = lax.optimization_barrier((mine, k_hi, k_lo, d_hi, d_lo))

        other = lax.ppermute(mine, "core", swap)
        mixed = mix_targets(core.reshape(1), mine, other, k_hi, k_lo)
        mixed = exchange(mixed, "near").sum(0)
        mixed = exchange(mixed.reshape(far, all_t // far, sub), "far")
        mixed = exchange(sum_copies(mixed), "far").reshape(all_t, sub)

        terms = score_docs(d_hi, d_lo, mixed)
        terms = terms.reshape(NEAR * cols, own, all_t)
        scores = exchange(terms, ("near", "chip", "core")).sum(0)
        place = lax.axis_index("chip") * 2 + core
        own_weight = lax.dynamic_slice_in_dim(doc_weight, place * own, own, 0)
        return scores * own_weight[:, None]

    in_specs = (P(row, col), P(row, col), P(row, None), P(row))
    return jax.shard_map(
        on_device, mesh=fine, in_specs=in_specs, out_specs=P(row + col, None), check_vma=False
    )
```

```python
import functools

import jax
import jax.numpy as jnp
from jax import lax
from jax.experimental import pallas as pl
from jax.experimental.pallas import tpu as pltpu
from jax.sharding import Mesh, PartitionSpec as P

NEAR = 4
VMEM = pl.BlockSpec(memory_space=pltpu.VMEM)
SMEM = pl.BlockSpec(memory_space=pltpu.SMEM)
PARAMS = pltpu.CompilerParams(vmem_limit_bytes=24 * 2**20)


def exchange(pieces, axis):
    return lax.all_to_all(pieces, axis, split_axis=0, concat_axis=0, tiled=True)


def split(x):
    hi = x.astype(jnp.bfloat16)
    return hi, (x - hi.astype(jnp.float32)).astype(jnp.bfloat16)


def dot3(left, right, left_dim, right_dim):
    def one(a, b):
        return lax.dot_general(
            a, b, (((left_dim,), (right_dim,)), ((), ())), preferred_element_type=jnp.float32
        )

    return one(left[0], right[0]) + (one(left[0], right[1]) + one(left[1], right[0]))


def cost(flops, size):
    return pl.CostEstimate(flops=flops, bytes_accessed=size, transcendentals=0)


def split_inverse(kernel_inv):
    n_i, n_j = kernel_inv.shape
    steps = 4

    def body(k_ref, hi_ref, lo_ref):
        hi_ref[...], lo_ref[...] = split(k_ref[...])

    block = pl.BlockSpec((n_i // steps, n_j), lambda s: (s, 0))
    half = jax.ShapeDtypeStruct((n_i, n_j), jnp.bfloat16)
    return pl.pallas_call(
        body,
        grid=(steps,),
        in_specs=[block],
        out_specs=[block, block],
        out_shape=[half, half],
        compiler_params=PARAMS,
        cost_estimate=cost(n_i * n_j * 4, n_i * n_j * 8),
        name="split_inverse",
    )(kernel_inv)


def mix_targets(both, k_hi, k_lo):
    cores, all_t, half = both.shape
    n_j = k_hi.shape[1]
    sub = n_j // NEAR

    def body(both_ref, hi_ref, lo_ref, out_ref):
        sides = [split(both_ref[s]) for s in range(cores)]
        for a in range(NEAR):
            cut = slice(a * sub, (a + 1) * sub)
            total = None
            for s, t in enumerate(sides):
                rows = slice(s * half, (s + 1) * half)
                part = dot3(t, (hi_ref[rows, cut], lo_ref[rows, cut]), 1, 0)
                total = part if total is None else total + part
            out_ref[a] = total

    return pl.pallas_call(
        body,
        in_specs=[VMEM, VMEM, VMEM],
        out_specs=VMEM,
        out_shape=jax.ShapeDtypeStruct((NEAR, all_t, sub), jnp.float32),
        compiler_params=PARAMS,
        cost_estimate=cost(6 * all_t * cores * half * n_j, 4 * 2**20),
        name="mix_targets",
    )(both, k_hi, k_lo)


def split_docs(place, blocks):
    near = len(blocks)
    each, width = blocks[0].shape

    def body(place_ref, *refs):
        hi_ref, lo_ref = refs[near:]
        for s in range(near):
            at = pl.ds(pl.multiple_of(place_ref[s] * each, each), each)
            hi_ref[at, :], lo_ref[at, :] = split(refs[s][...])

    half = jax.ShapeDtypeStruct((near * each, width), jnp.bfloat16)
    return pl.pallas_call(
        body,
        in_specs=[SMEM] + [VMEM] * near,
        out_specs=[VMEM, VMEM],
        out_shape=[half, half],
        compiler_params=PARAMS,
        cost_estimate=cost(4 * near * each * width, 8 * near * each * width),
        name="split_docs",
    )(place, *blocks)


def sum_copies(parts):
    n, some_t, sub = parts.shape

    def body(x_ref, out_ref):
        total = x_ref[0] + x_ref[1]
        for a in range(2, n):
            total = total + x_ref[a]
        for a in range(n):
            out_ref[a] = total

    return pl.pallas_call(
        body,
        in_specs=[VMEM],
        out_specs=VMEM,
        out_shape=jax.ShapeDtypeStruct(parts.shape, jnp.float32),
        compiler_params=PARAMS,
        cost_estimate=cost(n * some_t * sub, 8 * n * some_t * sub),
        name="sum_copies",
    )(parts)


def score_docs(d_hi, d_lo, mixed):
    n, width = d_hi.shape
    all_t = mixed.shape[0]

    def body(hi_ref, lo_ref, mixed_ref, out_ref):
        out_ref[...] = dot3((hi_ref[...], lo_ref[...]), split(mixed_ref[...]), 1, 1)

    return pl.pallas_call(
        body,
        in_specs=[VMEM] * 3,
        out_specs=VMEM,
        out_shape=jax.ShapeDtypeStruct((n, all_t), jnp.float32),
        compiler_params=PARAMS,
        cost_estimate=cost(6 * n * width * all_t, 2**20),
        name="score_docs",
    )(d_hi, d_lo, mixed)


def solution(mesh):
    rows, cols = mesh.shape["row"], mesh.shape["col"]
    far, chips = rows // NEAR, cols // 2
    names = ("far", "near", "chip", "core")
    fine = Mesh(mesh.devices.reshape(far, NEAR, chips, 2), names)
    row, col = ("far", "near"), ("chip", "core")

    def on_device(doc_feats, kernel_inv, target_feats, doc_weight):
        core = lax.axis_index("core")
        n_t, p = target_feats.shape
        n_i, n_j = kernel_inv.shape
        n_d = doc_feats.shape[0]
        half, sub, own = n_i // 2, n_j // NEAR, n_d // cols
        all_t = rows * n_t

        cut = target_feats.reshape(n_t, rows, 2, half)
        cut = lax.dynamic_index_in_dim(cut, core, 2, keepdims=False).transpose(1, 0, 2)
        mine = exchange(cut, row).reshape(all_t, half)
        k_hi, k_lo = split_inverse(kernel_inv)

        here = lax.axis_index("near")
        place = jnp.stack([here ^ s for s in range(NEAR)])
        blocks = []
        for s in range(NEAR):
            block = lax.dynamic_slice_in_dim(doc_feats, place[s] * sub, sub, 1)
            pairs = [(a, a ^ s) for a in range(NEAR)]
            blocks.append(lax.ppermute(block, "near", pairs) if s else block)
        d_hi, d_lo = split_docs(place, blocks)
        mine, k_hi, k_lo, d_hi, d_lo = lax.optimization_barrier((mine, k_hi, k_lo, d_hi, d_lo))

        both = lax.all_gather(mine, "core")
        mixed = mix_targets(both, k_hi, k_lo)
        mixed = exchange(mixed, "near").sum(0)
        mixed = exchange(mixed.reshape(far, all_t // far, sub), "far")
        mixed = exchange(sum_copies(mixed), "far").reshape(all_t, sub)

        terms = score_docs(d_hi, d_lo, mixed)
        terms = terms.reshape(NEAR * cols, own, all_t)
        scores = exchange(terms, ("near", "chip", "core")).sum(0)
        place = lax.axis_index("chip") * 2 + core
        own_weight = lax.dynamic_slice_in_dim(doc_weight, place * own, own, 0)
        return scores * own_weight[:, None]

    in_specs = (P(row, col), P(row, col), P(row, None), P(row))
    return jax.shard_map(
        on_device, mesh=fine, in_specs=in_specs, out_specs=P(row + col, None), check_vma=False
    )
```
